512 devices in a mesh: lag: 32 (over z_lo, x, core), row: 16 (over y, z_hi).
Axes of the slice: x: 4, y: 8, z: 8 (z_hi: 2, z_lo: 4; z = z_hi * 4 + z_lo), core: 2. Of those that a mesh axis runs over, the one named last changes fastest.
Arguments:
- z_blocks: bfloat16 [32, 192, 11, 128, 128], P('lag', 'row'), may hold values from -0.02734375 to 0.02734375
- block_cols: int32 [32, 192, 11], P('lag', 'row'), may hold values from 0 to 191, as said below
- history: bfloat16 [32, 24576, 128], P('lag', 'row'), may hold values from -6 to 6
- incident: bfloat16 [4, 24576, 128], P(None, 'row'), may hold values from -6 to 6
- near_inverse: float32 [192, 128, 128], P('row'), as said below
Outputs:
- current: bfloat16 [24576, 128], P('row')
The draws below stay inside these ranges and needn't reach their ends.
Inputs may be any that keep to these rules, and one draw needn't show every extreme that they name: `block_cols`: the 11 block columns of one block row of one lag are distinct and lie from (i // 12 - 1) * 12 to (i // 12 + 2) * 12 - 1, within 0 to 191. Each block of near_inverse has a diagonal near 1 to 2 and off-diagonal entries of order one over the square root of 128.
All inputs are finite; a program needn't handle non-finite values.
Results may differ from the reference program's by a relative error of at most 0.0054.
Values may be sent and summed in bfloat16 or wider, within the bound.
No kernel may reach another device: no remote copies, remote signals or barrier semaphores. Data moves between devices by JAX's collectives and lax.ppermute only.
A program may use at most 128 MiB of HBM per device.

```python
import jax
import jax.numpy as jnp
from jax import lax

B = 128
RB_DEV = 12
NZ = 11
RHS = 128
STEPS = 4
LAGS = 32
NBLK = 192
UNK = 24576


def draw_block_cols(key, part):
    key = jax.random.fold_in(key, 7)
    band = 3 * RB_DEV
    scores = jax.random.randint(key, (LAGS, NBLK, band), 0, 65536)
    offsets = jnp.arange(band, dtype=jnp.int32)
    starts = jnp.arange(NBLK, dtype=jnp.int32) // RB_DEV * RB_DEV - RB_DEV
    columns = starts[None, :, None] + offsets[None, None, :]
    valid = (columns >= 0) & (columns < NBLK)
    keyed = scores * band + offsets[None, None, :] + jnp.where(valid, 0, 65536 * band)
    order = jnp.argsort(keyed, axis=-1)
    chosen = jnp.take_along_axis(columns, order, axis=-1)[:, :, :NZ]
    return chosen.astype(jnp.int32)


def draw_near_inverse(key, part):
    key = jax.random.fold_in(key, 11)
    first, second = jax.random.split(key)
    diag = jax.random.uniform(first, (NBLK, B), jnp.float32, 1.0, 2.0)
    off = jax.random.normal(second, (NBLK, B, B), jnp.float32) * (0.5 / B ** 0.5)
    return (off + diag[:, :, None] * jnp.eye(B, dtype=jnp.float32)).astype(jnp.float32)


def block_levels(key, dims, shards, least, largest):
    gain, own = 1.0, jax.random.fold_in(key, 6)
    for position, shards_of in shards:
        steps = jnp.exp(jax.random.uniform(jax.random.fold_in(own, position), (shards_of,), jnp.float32, least / len(shards), largest / len(shards)))
        gain = gain * jnp.repeat(steps, dims[position] // shards_of).reshape([-1 if axis == position else 1 for axis in range(len(dims))])
    return gain


def bell_draw(key, dims, spread, limit, shards=(), held_as=jnp.bfloat16):
    factor_of = block_levels(key, dims, shards, -0.22, 0.18) if shards else 1.0
    result = jax.random.normal(key, dims, jnp.float32) * spread * factor_of
    return jnp.minimum(jnp.maximum(result, -limit), limit).astype(held_as)


def setup_inputs(seed: int = 0) -> dict:
    keys = jax.random.split(jax.random.key(seed), 6)
    z_blocks = bell_draw(keys[0], (LAGS, NBLK, NZ, B, B), (NZ * B * LAGS) ** -0.5, 0.02734375, ((0, 32), (1, 16)))
    block_cols = draw_block_cols(jax.random.fold_in(keys[5], 71), 0)
    history = bell_draw(keys[2], (LAGS, UNK, RHS), 1.0, 6.0, ((0, 32), (1, 16)))
    incident = bell_draw(keys[3], (STEPS, UNK, RHS), 1.0, 6.0, ((1, 16),))
    near_inverse = draw_near_inverse(jax.random.fold_in(keys[5], 71), 0)
    return dict(z_blocks=z_blocks, block_cols=block_cols, history=history, incident=incident, near_inverse=near_inverse)


def reference(z_blocks, block_cols, history, incident, near_inverse):
    computed = []
    for step in range(STEPS):
        older = [computed[step - 1 - k] for k in range(step)]
        if older:
            stack = jnp.concatenate([jnp.stack(older), history[:LAGS - step]], axis=0)
        else:
            stack = history

        def one_lag(total, pieces):
            zmat, cols, past = pieces
            tiles = past.reshape(NBLK, B, RHS)[cols]
            term = jnp.einsum("bjpq,bjqc->bpc", zmat.astype(jnp.float32), tiles.astype(jnp.float32))
            return total + term.reshape(UNK, RHS), None

        total, unused = lax.scan(one_lag, jnp.zeros((UNK, RHS), jnp.float32), (z_blocks, block_cols, stack))
        driven = incident[step].astype(jnp.float32) - total
        solved = jnp.einsum("bpq,bqc->bpc", near_inverse, driven.reshape(NBLK, B, RHS), precision=lax.Precision.HIGHEST)
        computed.append(solved.reshape(UNK, RHS).astype(jnp.bfloat16))
    return computed[-1]
```

```python
import functools

import jax
import jax.numpy as jnp
from jax import lax
from jax.experimental import pallas as pl
from jax.experimental.pallas import tpu as pltpu
from jax.sharding import PartitionSpec as P

CORES, XS = 2, 4
HALF = 64
AXES = ("lag", "row")


def coords(lag):
    return lag // (XS * CORES), lag // CORES % XS, lag % CORES


def lag_of(z, x, core):
    return (z * XS + x) * CORES + core


def pairs(lags, rows, target):
    out = []
    for lag in range(lags):
        for row in range(rows):
            goal = target(lag, row)
            if goal is not None and 0 <= goal[0] < lags and 0 <= goal[1] < rows:
                out.append((lag * rows + row, goal[0] * rows + goal[1]))
    return out


def send(value, target):
    lags, rows = lax.axis_size("lag"), lax.axis_size("row")
    return lax.ppermute(value, AXES, pairs(lags, rows, target))


def along_z(step, when):
    def target(lag, row):
        z, x, core = coords(lag)
        return (lag_of(z + step, x, core), row) if when(z, x) and z + step >= 0 else None
    return target


def along_x(step, when):
    def target(lag, row):
        z, x, core = coords(lag)
        return (lag_of(z, x + step, core), row) if when(z, x) else None
    return target


def other_core(lag, row):
    return lag ^ 1, row


def sparse_row(z_ref, row, tile, cols, count):
    total = None
    for first in range(0, count, 2):
        js = range(first, min(first + 2, count))
        left = [z_ref[row, j] for j in js]
        right = [tile(cols(j)) for j in js]
        if len(left) > 1:
            left, right = [jnp.concatenate(left, axis=1)], [jnp.concatenate(right, axis=0)]
        term = jnp.dot(left[0], right[0], preferred_element_type=jnp.float32)
        total = term if total is None else total + term
    return total


def low_lanes(shape):
    return lax.broadcasted_iota(jnp.int32, shape, len(shape) - 1) < HALF


def pack(first, second):
    low = low_lanes(first.shape)
    return (
        jnp.where(low, first, pltpu.roll(second, HALF, 1)),
        jnp.where(low, pltpu.roll(first, HALF, 1), second),
    )


def history_kernel(count, meta, z_ref, past_ref, keep_ref, send_ref):
    step = pl.program_id(0)
    core = meta[0]
    rows = []
    for part in range(2):
        base = 8 + (2 * step + part) * count
        rows.append(sparse_row(z_ref, part, lambda c: past_ref[c], lambda j: meta[base + j], count))
    low, high = pack(*rows)
    keep_ref[0] = jnp.where(core == 0, low, high)
    send_ref[0] = jnp.where(core == 0, high, low)


def history_partial(meta, zmat, past):
    blocks, count, width, unused = zmat.shape
    half = jax.ShapeDtypeStruct((blocks // 2, width, width), jnp.float32)
    spec = pl.BlockSpec((1, width, width), lambda i, meta: (i, 0, 0))
    return pl.pallas_call(
        functools.partial(history_kernel, count),
        out_shape=(half, half),
        grid_spec=pltpu.PrefetchScalarGridSpec(
            num_scalar_prefetch=1,
            grid=(blocks // 2,),
            in_specs=[
                pl.BlockSpec((2, count, width, width), lambda i, meta: (i, 0, 0, 0)),
                pl.BlockSpec(past.shape, lambda i, meta: (0, 0, 0)),
            ],
            out_specs=(spec, spec),
        ),
        compiler_params=pltpu.CompilerParams(vmem_limit_bytes=32 * 1024 * 1024),
        cost_estimate=pl.CostEstimate(
            flops=2 * blocks * count * width ** 3, bytes_accessed=zmat.size * 2, transcendentals=0
        ),
    )(meta, zmat, past)


def packed_rows(meta, z_ref, now_ref, step, count):
    rows = []
    for part in range(2):
        base = 8 + (2 * step + part) * count

        def tile(col):
            both = now_ref[col // 2]
            mine = low_lanes(both.shape) == (col % 2 == 0)
            return jnp.where(mine, both, jnp.zeros_like(both))

        total = sparse_row(z_ref, part, tile, lambda j: meta[base + j], count)
        rows.append(total + pltpu.roll(total, HALF, 1))
    return jnp.where(low_lanes(rows[0].shape), rows[0], rows[1])


def lag_kernel(count, meta, z_ref, now_ref, *rest):
    out_ref = rest[-1]
    step = pl.program_id(0)

    @pl.when(meta[1] != 0)
    def _():
        total = packed_rows(meta, z_ref, now_ref, step, count)
        if len(rest) == 2:
            total = total + rest[0][0]
        out_ref[0] = total


def lag_product(meta, zmat, now, *more):
    blocks, count, width, unused = zmat.shape
    spec = pl.BlockSpec((1, width, width), lambda i, meta: (i * meta[1], 0, 0))
    return pl.pallas_call(
        functools.partial(lag_kernel, count),
        out_shape=jax.ShapeDtypeStruct((blocks // 2, width, width), jnp.float32),
        grid_spec=pltpu.PrefetchScalarGridSpec(
            num_scalar_prefetch=1,
            grid=(blocks // 2,),
            in_specs=[
                pl.BlockSpec((2, count, width, width), lambda i, meta: (i * meta[1], 0, 0, 0)),
                pl.BlockSpec(now.shape, lambda i, meta: (0, 0, 0)),
            ] + [spec] * len(more),
            out_specs=spec,
        ),
        compiler_params=pltpu.CompilerParams(vmem_limit_bytes=32 * 1024 * 1024),
    )(meta, zmat, now, *more)


def step_kernel(count, product, old, meta, *refs):
    refs = list(refs)
    incident_ref, summed_ref, inverse_ref = refs[:3]
    out_ref = refs[-1]
    step = pl.program_id(0)

    @pl.when(meta[1] != 0)
    def _():
        parts = []
        for part in range(2):
            parts.append(incident_ref[part].astype(jnp.float32))
        low, high = pack(*parts)
        driven = jnp.where(meta[0] == 0, low, high) - summed_ref[0]
        if old:
            driven = driven - refs[-2][0]
        if product:
            driven = driven - packed_rows(meta, refs[3], refs[4], step, count)
        solved = []
        for part in range(2):
            solved.append(
                jnp.dot(
                    inverse_ref[part], driven,
                    precision=lax.Precision.HIGHEST, preferred_element_type=jnp.float32,
                )
            )
        out_ref[0] = jnp.where(low_lanes(driven.shape), solved[0], solved[1]).astype(out_ref.dtype)


def solve_step(meta, incident, summed, inverse, zmat=None, now=None, old=None):
    blocks, width, unused = inverse.shape
    count = 1 if zmat is None else zmat.shape[1]
    spec = pl.BlockSpec((1, width, width), lambda i, meta: (i * meta[1], 0, 0))
    twice = pl.BlockSpec((2, width, width), lambda i, meta: (i * meta[1], 0, 0))
    args, specs = [incident, summed, inverse], [twice, spec, twice]
    if zmat is not None:
        args += [zmat, now]
        specs += [
            pl.BlockSpec((2, count, width, width), lambda i, meta: (i * meta[1], 0, 0, 0)),
            pl.BlockSpec(now.shape, lambda i, meta: (0, 0, 0)),
        ]
    if old is not None:
        args.append(old)
        specs.append(spec)
    return pl.pallas_call(
        functools.partial(step_kernel, count, zmat is not None, old is not None),
        out_shape=jax.ShapeDtypeStruct((blocks // 2, width, width), jnp.bfloat16),
        grid_spec=pltpu.PrefetchScalarGridSpec(
            num_scalar_prefetch=1, grid=(blocks // 2,), in_specs=specs, out_specs=spec
        ),
        compiler_params=pltpu.CompilerParams(vmem_limit_bytes=32 * 1024 * 1024),
    )(meta, *args)


def unpack_kernel(meta, mine_ref, other_ref, out_ref):
    mine, other = mine_ref[0].astype(jnp.float32), other_ref[0].astype(jnp.float32)
    low = jnp.where(meta[0] == 0, mine, other)
    high = jnp.where(meta[0] == 0, other, mine)
    first, second = pack(low, high)
    out_ref[0] = first.astype(out_ref.dtype)
    out_ref[1] = second.astype(out_ref.dtype)


def unpack(meta, mine, other):
    count, width, unused = mine.shape
    spec = pl.BlockSpec((1, width, width), lambda i, meta: (i, 0, 0))
    return pl.pallas_call(
        unpack_kernel,
        out_shape=jax.ShapeDtypeStruct((2 * count, width, width), mine.dtype),
        grid_spec=pltpu.PrefetchScalarGridSpec(
            num_scalar_prefetch=1,
            grid=(count,),
            in_specs=[spec, spec],
            out_specs=pl.BlockSpec((2, width, width), lambda i, meta: (i, 0, 0)),
        ),
    )(meta, mine, other)


def swap_rows(lag, row):
    return lag, row ^ 1


def next_chip(lag, row):
    return lag, (row + 2 if row % 2 == 0 else row - 2)


def on_root(step):
    def target(lag, row):
        return (lag, row + step) if lag < CORES else None
    return target


def reduced(keep, extra):
    total = keep + send(extra, other_core)
    for move in (
        along_x(-1, lambda z, x: x % 2 == 1),
        along_x(-2, lambda z, x: x == 2),
        along_z(-1, lambda z, x: x == 0 and z % 2 == 1),
        along_z(-2, lambda z, x: x == 0 and z == 2),
    ):
        total = total + send(total.astype(jnp.bfloat16), move).astype(jnp.float32)
    return total


def spread(value, z_pos, x_pos):
    for move, got in (
        (along_z(2, lambda z, x: x == 0 and z == 0), (x_pos == 0) & (z_pos == 2)),
        (along_z(1, lambda z, x: x == 0 and z % 2 == 0), (x_pos == 0) & (z_pos % 2 == 1)),
        (along_x(2, lambda z, x: x == 0), x_pos == 2),
        (along_x(1, lambda z, x: x % 2 == 0), x_pos % 2 == 1),
    ):
        value = jnp.where(got, send(value, move), value)
    return value


def per_device(z_blocks, block_cols, history, incident, near_inverse):
    blocks, width, unused = near_inverse.shape
    zmat = z_blocks[0]
    count = zmat.shape[1]
    lag_pos = lax.axis_index("lag")
    row_pos = lax.axis_index("row")
    z_pos, x_pos, core = coords(lag_pos)
    root = (lag_pos < CORES).astype(jnp.int32)
    own = history[0].reshape(blocks, width, width)
    fields = incident.reshape(incident.shape[0], blocks, width, width)

    cols = block_cols[0].reshape(-1) - (row_pos - 1) * blocks
    group, inside = cols // blocks, cols % blocks
    even = row_pos % 2 == 0
    slot = jnp.where(group == 1, 0, jnp.where((group == 2) == even, 1, 2))
    flags = jnp.zeros((8,), jnp.int32).at[0].set(core).at[1].set(root)
    history_meta = jnp.concatenate([flags, slot * blocks + inside])

    def to_root(lag, row):
        return (lag ^ 1, row) if lag < CORES else None

    def third(lag, row):
        return (0, row) if lag == CORES else None

    def shared(lag, row):
        return (1, row) if lag == 0 else None

    def gathered(value):
        swapped = send(value, to_root)
        first = jnp.where(lag_pos == 0, value, swapped)
        second = jnp.where(lag_pos == 0, swapped, value)
        got = send(value, third)
        last = jnp.where(lag_pos == 0, got, send(got, shared))
        return first, second, last

    near = send(own, swap_rows)
    far = send(near, next_chip)
    past = jnp.concatenate([own, near, far], axis=0)

    z_lags = gathered(zmat)
    metas = [jnp.concatenate([flags, c]) for c in gathered(cols)]

    sums = []
    for step in range(4):
        keep, extra = history_partial(history_meta, zmat, past)
        sums.append(reduced(keep, extra))
        if step < 3:
            past = send(past, lambda lag, row: (lag + 1, row))

    def wide(value):
        below = send(value, on_root(1))
        above = send(value, on_root(-1))
        return jnp.concatenate([below, value, above], axis=0)

    c0 = wide(solve_step(metas[0], fields[0], sums[0], near_inverse))
    c1 = wide(solve_step(metas[0], fields[1], sums[1], near_inverse, z_lags[0], c0))
    old = lag_product(metas[1], z_lags[1], c0)
    c2 = wide(solve_step(metas[0], fields[2], sums[2], near_inverse, z_lags[0], c1, old))
    old = lag_product(metas[2], z_lags[2], c0)
    old = lag_product(metas[1], z_lags[1], c1, old)
    c3 = solve_step(metas[0], fields[3], sums[3], near_inverse, z_lags[0], c2, old)
    c3 = spread(c3, z_pos, x_pos)
    out = unpack(history_meta, c3, send(c3, other_core))
    return out.reshape(blocks * width, width)


def solution(mesh):
    return jax.shard_map(
        per_device,
        mesh=mesh,
        in_specs=(
            P("lag", "row", None, None, None),
            P("lag", "row", None),
            P("lag", "row", None),
            P(None, "row", None),
            P("row", None, None),
        ),
        out_specs=P("row", None),
        check_vma=False,
    )
```

```python
import functools

import jax
import jax.numpy as jnp
from jax import lax
from jax.experimental import pallas as pl
from jax.experimental.pallas import tpu as pltpu
from jax.sharding import PartitionSpec as P

CORES, XS = 2, 4
HALF = 64
AXES = ("lag", "row")


def coords(lag):
    return lag // (XS * CORES), lag // CORES % XS, lag % CORES


def lag_of(z, x, core):
    return (z * XS + x) * CORES + core


def pairs(lags, rows, target):
    out = []
    for lag in range(lags):
        for row in range(rows):
            goal = target(lag, row)
            if goal is not None and 0 <= goal[0] < lags and 0 <= goal[1] < rows:
                out.append((lag * rows + row, goal[0] * rows + goal[1]))
    return out


def send(value, target):
    lags, rows = lax.axis_size("lag"), lax.axis_size("row")
    return lax.ppermute(value, AXES, pairs(lags, rows, target))


def along_z(step, when):
    def target(lag, row):
        z, x, core = coords(lag)
        return (lag_of(z + step, x, core), row) if when(z, x) and z + step >= 0 else None
    return target


def along_x(step, when):
    def target(lag, row):
        z, x, core = coords(lag)
        return (lag_of(z, x + step, core), row) if when(z, x) else None
    return target


def other_core(lag, row):
    return lag ^ 1, row


def sparse_row(z_ref, row, tile, cols, count):
    left = jnp.concatenate([z_ref[row, j] for j in range(count)], axis=1)
    right = jnp.concatenate([tile(cols(j)) for j in range(count)], axis=0)
    return jnp.dot(left, right, preferred_element_type=jnp.float32)


def low_lanes(shape):
    return lax.broadcasted_iota(jnp.int32, shape, len(shape) - 1) < HALF


def pack(first, second):
    low = low_lanes(first.shape)
    return (
        jnp.where(low, first, pltpu.roll(second, HALF, 1)),
        jnp.where(low, pltpu.roll(first, HALF, 1), second),
    )


VMEM = pl.BlockSpec(memory_space=pltpu.VMEM)
SMEM = pl.BlockSpec(memory_space=pltpu.SMEM)
HBM = pl.BlockSpec(memory_space=pl.ANY)
CHUNKS = 3
CORE, ROOT, NEXT, HEAD = 0, 1, 2, 8


def chunk_copies(source, buffer, sems):
    size = source.shape[0] // CHUNKS
    return [
        pltpu.make_async_copy(
            source.at[pl.ds(c * size, size)], buffer.at[pl.ds(c * size, size)], sems.at[c]
        )
        for c in range(CHUNKS)
    ]


def z_scratch(zmat):
    return [pltpu.VMEM(zmat.shape, zmat.dtype), pltpu.SemaphoreType.DMA((CHUNKS,))]


def call(kernel, out_shape, in_specs, scratch, flops, *args):
    outs = len(out_shape) if isinstance(out_shape, tuple) else 0
    return pl.pallas_call(
        kernel,
        out_shape=out_shape,
        in_specs=in_specs,
        out_specs=(VMEM,) * outs if outs else VMEM,
        scratch_shapes=scratch,
        compiler_params=pltpu.CompilerParams(vmem_limit_bytes=40 * 1024 * 1024),
        cost_estimate=pl.CostEstimate(flops=flops, bytes_accessed=5 * 10 ** 6, transcendentals=0),
    )(*args)


def history_kernel(meta, z_ref, past_ref, keep_ref, send_ref, buffer, sems):
    count = z_ref.shape[1]
    copies = chunk_copies(z_ref, buffer, sems)
    for copy in copies:
        copy.start()
    groups = z_ref.shape[0] // CHUNKS
    for pair in range(z_ref.shape[0] // 2):
        if 2 * pair % groups == 0:
            copies[2 * pair // groups].wait()
        rows = []
        for row in (2 * pair, 2 * pair + 1):
            base = HEAD + row * count
            rows.append(
                sparse_row(buffer, row, lambda c: past_ref[c], lambda j: meta[base + j], count)
            )
        low, high = pack(*rows)
        keep_ref[pair] = jnp.where(meta[CORE] == 0, low, high)
        send_ref[pair] = jnp.where(meta[CORE] == 0, high, low)


def history_partial(meta, zmat, past):
    blocks, count, width, unused = zmat.shape
    half = jax.ShapeDtypeStruct((blocks // 2, width, width), jnp.float32)
    return call(
        history_kernel, (half, half), [SMEM, HBM, VMEM], z_scratch(zmat),
        2 * blocks * count * width ** 3, meta, zmat, past,
    )


def load_lag(first, meta, mine_ref, swapped_ref, buffer, sems):
    mine = chunk_copies(mine_ref, buffer, sems)
    swapped = chunk_copies(swapped_ref, buffer, sems)
    direct = (meta[CORE] == 0) == first

    @pl.when(direct)
    def _():
        for copy in mine:
            copy.start()

    @pl.when(jnp.logical_not(direct))
    def _():
        for copy in swapped:
            copy.start()

    return mine


def packed_rows(meta, buffer, now_ref, pair, count):
    rows = []
    for row in (2 * pair, 2 * pair + 1):
        base = HEAD + row * count

        def tile(col):
            both = now_ref[col // 2]
            mine = low_lanes(both.shape) == (col % 2 == 0)
            return jnp.where(mine, both, jnp.zeros_like(both))

        total = sparse_row(buffer, row, tile, lambda j: meta[base + j], count)
        rows.append(total + pltpu.roll(total, HALF, 1))
    return jnp.where(low_lanes(rows[0].shape), rows[0], rows[1])


def lag_kernel(first, flag, meta, mine_ref, swapped_ref, now_ref, *rest):
    more, (out_ref, buffer, sems) = rest[:-3], rest[-3:]
    blocks, count = mine_ref.shape[0], mine_ref.shape[1]

    @pl.when(meta[flag] != 0)
    def _():
        copies = load_lag(first, meta, mine_ref, swapped_ref, buffer, sems)
        for copy in copies:
            copy.wait()
        for pair in range(blocks // 2):
            total = packed_rows(meta, buffer, now_ref, pair, count)
            for ref in more:
                total = total + ref[pair].astype(jnp.float32)
            out_ref[pair] = total.astype(out_ref.dtype)


def lag_product(first, flag, dtype, meta, mine, swapped, now, *more):
    blocks, count, width, unused = mine.shape
    return call(
        functools.partial(lag_kernel, first, flag),
        jax.ShapeDtypeStruct((blocks // 2, width, width), dtype),
        [SMEM, HBM, HBM, VMEM] + [VMEM] * len(more), z_scratch(mine),
        2 * blocks * count * width ** 3, meta, mine, swapped, now, *more,
    )


def step_kernel(product, old, meta, incident_ref, summed_ref, inverse_ref, *refs):
    refs = list(refs)
    if product:
        buffer, sems = refs[-2:]
        refs = refs[:-2]
    out_ref = refs.pop()

    @pl.when(meta[ROOT] != 0)
    def _():
        if product:
            copies = load_lag(True, meta, refs[0], refs[1], buffer, sems)
            groups = buffer.shape[0] // CHUNKS
        for pair in range(summed_ref.shape[0]):
            low, high = pack(*(incident_ref[2 * pair + p].astype(jnp.float32) for p in range(2)))
            driven = jnp.where(meta[CORE] == 0, low, high) - summed_ref[pair]
            if old:
                driven = driven - refs[-1][pair]
            if product:
                if 2 * pair % groups == 0:
                    copies[2 * pair // groups].wait()
                driven = driven - packed_rows(meta, buffer, refs[2], pair, buffer.shape[1])
            solved = [
                jnp.dot(
                    inverse_ref[2 * pair + p], driven,
                    precision=lax.Precision.HIGHEST, preferred_element_type=jnp.float32,
                )
                for p in range(2)
            ]
            out_ref[pair] = jnp.where(low_lanes(driven.shape), *solved).astype(out_ref.dtype)


def solve_step(meta, incident, summed, inverse, mine=None, swapped=None, now=None, old=None):
    blocks, width, unused = inverse.shape
    args, specs, scratch = [meta, incident, summed, inverse], [SMEM, VMEM, VMEM, VMEM], []
    if mine is not None:
        args += [mine, swapped, now]
        specs += [HBM, HBM, VMEM]
        scratch = z_scratch(mine)
    if old is not None:
        args.append(old)
        specs.append(VMEM)
    return call(
        functools.partial(step_kernel, mine is not None, old is not None),
        jax.ShapeDtypeStruct((blocks // 2, width, width), jnp.bfloat16),
        specs, scratch, 10 ** 9, *args,
    )


def unpack_kernel(meta, mine_ref, other_ref, out_ref):
    for pair in range(mine_ref.shape[0]):
        mine, other = mine_ref[pair].astype(jnp.float32), other_ref[pair].astype(jnp.float32)
        low = jnp.where(meta[CORE] == 0, mine, other)
        high = jnp.where(meta[CORE] == 0, other, mine)
        first, second = pack(low, high)
        out_ref[2 * pair] = first.astype(out_ref.dtype)
        out_ref[2 * pair + 1] = second.astype(out_ref.dtype)


def unpack(meta, mine, other):
    count, width, unused = mine.shape
    return call(
        unpack_kernel, jax.ShapeDtypeStruct((2 * count, width, width), mine.dtype),
        [SMEM, VMEM, VMEM], [], 10 ** 6, meta, mine, other,
    )


def swap_rows(lag, row):
    return lag, row ^ 1


def next_chip(lag, row):
    return lag, (row + 2 if row % 2 == 0 else row - 2)


def on_root(step):
    def target(lag, row):
        return (lag, row + step) if lag < CORES else None
    return target


def reduced(keep, extra):
    total = keep + send(extra, other_core)
    for move in (
        along_x(-1, lambda z, x: x % 2 == 1),
        along_x(-2, lambda z, x: x == 2),
        along_z(-1, lambda z, x: x == 0 and z % 2 == 1),
        along_z(-2, lambda z, x: x == 0 and z == 2),
    ):
        total = total + send(total.astype(jnp.bfloat16), move).astype(jnp.float32)
    return total


def spread(value, z_pos, x_pos):
    for move, got in (
        (along_z(2, lambda z, x: x == 0 and z == 0), (x_pos == 0) & (z_pos == 2)),
        (along_z(1, lambda z, x: x == 0 and z % 2 == 0), (x_pos == 0) & (z_pos % 2 == 1)),
        (along_x(2, lambda z, x: x == 0), x_pos == 2),
        (along_x(1, lambda z, x: x % 2 == 0), x_pos % 2 == 1),
    ):
        value = jnp.where(got, send(value, move), value)
    return value


def per_device(z_blocks, block_cols, history, incident, near_inverse):
    blocks, width, unused = near_inverse.shape
    zmat = z_blocks[0]
    lag_pos = lax.axis_index("lag")
    row_pos = lax.axis_index("row")
    z_pos, x_pos, core = coords(lag_pos)
    own = history[0].reshape(blocks, width, width)
    fields = [f.reshape(blocks, width, width) for f in incident]

    cols = block_cols[0].reshape(-1) - (row_pos - 1) * blocks
    group, inside = cols // blocks, cols % blocks
    even = row_pos % 2 == 0
    slot = jnp.where(group == 1, 0, jnp.where((group == 2) == even, 1, 2))
    chip = lag_pos // CORES
    flags = jnp.stack([core, chip == 0, chip == 1] + [0] * (HEAD - 3)).astype(jnp.int32)
    history_meta = jnp.concatenate([flags, slot * blocks + inside])

    def first_chips(lag, row):
        return (lag ^ 1, row) if lag < 2 * CORES else None

    near = send(own, swap_rows)
    swapped_cols = send(cols, first_chips)
    swapped = send(zmat, first_chips)
    far = send(near, next_chip)
    past = jnp.concatenate([own, near, far], axis=0)
    first_meta = jnp.concatenate([flags, jnp.where(core == 0, cols, swapped_cols)])
    second_meta = jnp.concatenate([flags, jnp.where(core == 0, swapped_cols, cols)])

    sums = []
    for step in range(4):
        keep, extra = history_partial(history_meta, zmat, past)
        sums.append(reduced(keep, extra))
        if step < 3:
            past = send(past, lambda lag, row: (lag + 1, row))

    def wide(value):
        below = send(value, on_root(1))
        above = send(value, on_root(-1))
        return jnp.concatenate([below, value, above], axis=0)

    lags = (zmat, swapped)
    c0 = wide(solve_step(first_meta, fields[0], sums[0], near_inverse))
    third = send(c0, along_x(1, lambda z, x: z == 0 and x == 0))
    third = lag_product(True, NEXT, jnp.bfloat16, first_meta, *lags, third)
    third = send(third, along_x(-1, lambda z, x: z == 0 and x == 1))
    c1 = wide(solve_step(first_meta, fields[1], sums[1], near_inverse, *lags, c0))
    old = lag_product(False, ROOT, jnp.float32, second_meta, *lags, c0)
    c2 = wide(solve_step(first_meta, fields[2], sums[2], near_inverse, *lags, c1, old))
    old = lag_product(False, ROOT, jnp.float32, second_meta, *lags, c1, third)
    c3 = solve_step(first_meta, fields[3], sums[3], near_inverse, *lags, c2, old)
    c3 = spread(c3, z_pos, x_pos)
    out = unpack(history_meta, c3, send(c3, other_core))
    return out.reshape(blocks * width, width)


def solution(mesh):
    return jax.shard_map(
        per_device,
        mesh=mesh,
        in_specs=(
            P("lag", "row", None, None, None),
            P("lag", "row", None),
            P("lag", "row", None),
            P(None, "row", None),
            P("row", None, None),
        ),
        out_specs=P("row", None),
        check_vma=False,
    )
```

```python
import functools

import jax
import jax.numpy as jnp
from jax import lax
from jax.experimental import pallas as pl
from jax.experimental.pallas import tpu as pltpu
from jax.sharding import PartitionSpec as P

CORES, XS = 2, 4
HALF = 64
AXES = ("lag", "row")


def coords(lag):
    return lag // (XS * CORES), lag // CORES % XS, lag % CORES


def lag_of(z, x, core):
    return (z * XS + x) * CORES + core


def pairs(lags, rows, target):
    out = []
    for lag in range(lags):
        for row in range(rows):
            goal = target(lag, row)
            if goal is not None and 0 <= goal[0] < lags and 0 <= goal[1] < rows:
                out.append((lag * rows + row, goal[0] * rows + goal[1]))
    return out


def send(value, target):
    lags, rows = lax.axis_size("lag"), lax.axis_size("row")
    return lax.ppermute(value, AXES, pairs(lags, rows, target))


def along_z(step, when):
    def target(lag, row):
        z, x, core = coords(lag)
        return (lag_of(z + step, x, core), row) if when(z, x) and z + step >= 0 else None
    return target


def along_x(step, when):
    def target(lag, row):
        z, x, core = coords(lag)
        return (lag_of(z, x + step, core), row) if when(z, x) else None
    return target


def other_core(lag, row):
    return lag ^ 1, row


def sparse_row(z_ref, row, tile, cols, count):
    left = jnp.concatenate([z_ref[row, j] for j in range(count)], axis=1)
    right = jnp.concatenate([tile(cols(j)) for j in range(count)], axis=0)
    return jnp.dot(left, right, preferred_element_type=jnp.float32)


def low_lanes(shape):
    return lax.broadcasted_iota(jnp.int32, shape, len(shape) - 1) < HALF


def pack(first, second):
    low = low_lanes(first.shape)
    return (
        jnp.where(low, first, pltpu.roll(second, HALF, 1)),
        jnp.where(low, pltpu.roll(first, HALF, 1), second),
    )


VMEM = pl.BlockSpec(memory_space=pltpu.VMEM)
SMEM = pl.BlockSpec(memory_space=pltpu.SMEM)
CORE, ROOT, NEXT, HEAD = 0, 1, 2, 8


def call(kernel, out_shape, flops, meta, *args):
    outs = len(out_shape) if isinstance(out_shape, tuple) else 0
    return pl.pallas_call(
        kernel,
        out_shape=out_shape,
        in_specs=[SMEM] + [VMEM] * len(args),
        out_specs=(VMEM,) * outs if outs else VMEM,
        compiler_params=pltpu.CompilerParams(vmem_limit_bytes=14 * 1024 * 1024),
        cost_estimate=pl.CostEstimate(flops=flops, bytes_accessed=5 * 10 ** 6, transcendentals=0),
    )(meta, *args)


def history_kernel(meta, z_ref, *refs):
    pasts, (keep_ref, send_ref) = refs[:-2], refs[-2:]
    blocks, count, width, unused = z_ref.shape

    def tile(col):
        return jnp.concatenate([past[col] for past in pasts], axis=1)

    for pair in range(blocks // 2):
        rows = []
        for row in (2 * pair, 2 * pair + 1):
            base = HEAD + row * count
            rows.append(sparse_row(z_ref, row, tile, lambda j: meta[base + j], count))
        for number in range(len(pasts)):
            lanes = slice(number * width, (number + 1) * width)
            low, high = pack(*(row[:, lanes] for row in rows))
            place = number * (blocks // 2) + pair
            keep_ref[place] = jnp.where(meta[CORE] == 0, low, high)
            send_ref[place] = jnp.where(meta[CORE] == 0, high, low)


def history_partial(meta, zmat, *pasts):
    blocks, count, width, unused = zmat.shape
    half = jax.ShapeDtypeStruct((len(pasts) * blocks // 2, width, width), jnp.float32)
    return call(
        history_kernel, (half, half), 2 * len(pasts) * blocks * count * width ** 3,
        meta, zmat, *pasts,
    )


def packed_rows(meta, z_ref, now_ref, pair):
    count = z_ref.shape[1]
    rows = []
    for row in (2 * pair, 2 * pair + 1):
        base = HEAD + row * count

        def tile(col):
            both = now_ref[col // 2]
            mine = low_lanes(both.shape) == (col % 2 == 0)
            return jnp.where(mine, both, jnp.zeros_like(both))

        total = sparse_row(z_ref, row, tile, lambda j: meta[base + j], count)
        rows.append(total + pltpu.roll(total, HALF, 1))
    return jnp.where(low_lanes(rows[0].shape), rows[0], rows[1])


def lag_kernel(flag, meta, z_ref, now_ref, *rest):
    more, out_ref = rest[:-1], rest[-1]

    @pl.when(meta[flag] != 0)
    def _():
        for pair in range(out_ref.shape[0]):
            total = packed_rows(meta, z_ref, now_ref, pair)
            for ref in more:
                total = total + ref[pair].astype(jnp.float32)
            out_ref[pair] = total.astype(out_ref.dtype)


def lag_product(flag, dtype, meta, zmat, now, *more):
    blocks, count, width, unused = zmat.shape
    return call(
        functools.partial(lag_kernel, flag),
        jax.ShapeDtypeStruct((blocks // 2, width, width), dtype),
        2 * blocks * count * width ** 3, meta, zmat, now, *more,
    )


def step_kernel(place, meta, incident_ref, summed_ref, inverse_ref, *refs):
    out_ref = refs[-1]

    @pl.when(meta[ROOT] != 0)
    def _():
        for pair in range(out_ref.shape[0]):
            low, high = pack(*(incident_ref[2 * pair + p].astype(jnp.float32) for p in range(2)))
            driven = jnp.where(meta[CORE] == 0, low, high) - summed_ref[place * out_ref.shape[0] + pair]
            if len(refs) > 1:
                driven = driven - packed_rows(meta, refs[0], refs[1], pair)
            for old in refs[2:-1]:
                driven = driven - old[pair].astype(jnp.float32)
            solved = [
                jnp.dot(
                    inverse_ref[2 * pair + p], driven,
                    precision=lax.Precision.HIGHEST, preferred_element_type=jnp.float32,
                )
                for p in range(2)
            ]
            out_ref[pair] = jnp.where(low_lanes(driven.shape), *solved).astype(out_ref.dtype)


def solve_step(place, meta, incident, summed, inverse, *more):
    blocks, width, unused = inverse.shape
    return call(
        functools.partial(step_kernel, place),
        jax.ShapeDtypeStruct((blocks // 2, width, width), jnp.bfloat16),
        10 ** 9, meta, incident, summed, inverse, *more,
    )


def unpack_kernel(meta, mine_ref, other_ref, out_ref):
    for pair in range(mine_ref.shape[0]):
        mine, other = mine_ref[pair].astype(jnp.float32), other_ref[pair].astype(jnp.float32)
        low = jnp.where(meta[CORE] == 0, mine, other)
        high = jnp.where(meta[CORE] == 0, other, mine)
        first, second = pack(low, high)
        out_ref[2 * pair] = first.astype(out_ref.dtype)
        out_ref[2 * pair + 1] = second.astype(out_ref.dtype)


def unpack(meta, mine, other):
    count, width, unused = mine.shape
    return call(
        unpack_kernel, jax.ShapeDtypeStruct((2 * count, width, width), mine.dtype),
        10 ** 6, meta, mine, other,
    )


def swap_rows(lag, row):
    return lag, row ^ 1


def next_chip(lag, row):
    return lag, (row + 2 if row % 2 == 0 else row - 2)


def on_root(step):
    def target(lag, row):
        return (lag, row + step) if lag < CORES else None
    return target


def after(value, *done):
    return lax.optimization_barrier((value,) + done)[0]


TREE = (
    along_x(-1, lambda z, x: x % 2 == 1),
    along_x(-2, lambda z, x: x == 2),
    along_z(-1, lambda z, x: x == 0 and z % 2 == 1),
    along_z(-2, lambda z, x: x == 0 and z == 2),
)


def halves(pieces):
    keep, extra = pieces
    return keep + send(extra, other_core)


def stage(total, number):
    moved = send(total.astype(jnp.bfloat16), TREE[number])
    return total + moved.astype(jnp.float32)


def spread(value, got):
    moves = (
        along_z(2, lambda z, x: x == 0 and z == 0),
        along_z(1, lambda z, x: x == 0 and z % 2 == 0),
        along_x(2, lambda z, x: x == 0),
        along_x(1, lambda z, x: x % 2 == 0),
    )
    for move, here in zip(moves, got):
        value = jnp.where(here, send(value, move), value)
    return value


def per_device(z_blocks, block_cols, history, incident, near_inverse):
    blocks, width, unused = near_inverse.shape
    zmat = z_blocks[0]
    lag_pos = lax.axis_index("lag")
    row_pos = lax.axis_index("row")
    z_pos, x_pos, core = coords(lag_pos)
    own = history[0].reshape(blocks, width, width)
    fields = [f.reshape(blocks, width, width) for f in incident]

    cols = block_cols[0].reshape(-1) - (row_pos - 1) * blocks
    group, inside = cols // blocks, cols % blocks
    even = row_pos % 2 == 0
    slot = jnp.where(group == 1, 0, jnp.where((group == 2) == even, 1, 2))
    chip = lag_pos // CORES
    flags = jnp.stack([core, chip == 0, chip == 1] + [0] * (HEAD - 3)).astype(jnp.int32)
    history_meta = jnp.concatenate([flags, slot * blocks + inside])

    def first_chips(lag, row):
        return (lag ^ 1, row) if lag < 2 * CORES else None

    def next_lag(past):
        return send(past, lambda lag, row: (lag + 1, row))

    def wide(value):
        below = send(value, on_root(1))
        above = send(value, on_root(-1))
        return jnp.concatenate([below, value, above], axis=0)

    near = send(own, swap_rows)
    swapped_cols = send(cols, first_chips)
    swapped = send(zmat, first_chips)
    first = jnp.where(core == 0, zmat, swapped)
    second = jnp.where(core == 0, swapped, zmat)
    first_meta = jnp.concatenate([flags, jnp.where(core == 0, cols, swapped_cols)])
    second_meta = jnp.concatenate([flags, jnp.where(core == 0, swapped_cols, cols)])
    x_zero = x_pos == 0
    got = [x_zero & (z_pos == 2), x_zero & (z_pos % 2 == 1), x_pos == 2, x_pos % 2 == 1]
    near, history_meta, first_meta, second_meta, got, first, second = lax.optimization_barrier(
        (near, history_meta, first_meta, second_meta, got, first, second)
    )
    far = send(near, next_chip)
    past0 = jnp.concatenate([own, near, far], axis=0)
    past1 = next_lag(past0)
    past2 = next_lag(past1)
    past3 = next_lag(past2)

    def partial(past):
        return history_partial(history_meta, zmat, past)

    a = stage(halves(partial(past0)), 0)
    part1 = partial(past1)
    a = stage(after(a, part1[0]), 1)
    b = halves(part1)
    a = stage(after(a, b), 2)
    b = stage(b, 0)
    part2 = partial(after(past2, a))
    a = stage(after(a, b), 3)
    b = stage(b, 1)
    c = halves(part2)
    current0 = solve_step(0, first_meta, fields[0], after(a, b, part2[0]), near_inverse)

    b = stage(after(b, current0), 2)
    c0 = wide(current0)
    c = stage(after(c, current0), 0)
    part3 = partial(after(past3, current0))
    b = stage(b, 3)
    c = stage(c, 1)
    d = halves(part3)
    current1 = solve_step(0, first_meta, fields[1], after(b, c, d), near_inverse, first, c0)

    c = stage(after(c, current1), 2)
    d = stage(after(d, current1), 0)
    c1 = wide(current1)
    third = send(after(c0, c, d), along_x(1, lambda z, x: z == 0 and x == 0))
    old = lag_product(ROOT, jnp.float32, second_meta, second, after(c0, c, d))
    c = stage(c, 3)
    d = stage(d, 1)
    current2 = solve_step(0, first_meta, fields[2], after(c, d), near_inverse, first, c1, old)

    third = lag_product(NEXT, jnp.bfloat16, first_meta, first, after(third, current2))
    third = send(third, along_x(-1, lambda z, x: z == 0 and x == 1))
    d = stage(after(d, current2), 2)
    c2 = wide(current2)
    old = lag_product(ROOT, jnp.float32, second_meta, second, after(c1, d))
    d = stage(d, 3)
    c3 = solve_step(0, first_meta, fields[3], d, near_inverse, first, c2, old, third)
    c3 = spread(c3, got)
    out = unpack(history_meta, c3, send(c3, other_core))
    return out.reshape(blocks * width, width)


def solution(mesh):
    return jax.shard_map(
        per_device,
        mesh=mesh,
        in_specs=(
            P("lag", "row", None, None, None),
            P("lag", "row", None),
            P("lag", "row", None),
            P(None, "row", None),
            P("row", None, None),
        ),
        out_specs=P("row", None),
        check_vma=False,
    )
```

```python
import functools

import jax
import jax.numpy as jnp
from jax import lax
from jax.experimental import pallas as pl
from jax.experimental.pallas import tpu as pltpu
from jax.sharding import PartitionSpec as P

CORES, XS = 2, 4
HALF = 64
AXES = ("lag", "row")


def coords(lag):
    return lag // (XS * CORES), lag // CORES % XS, lag % CORES


def lag_of(z, x, core):
    return (z * XS + x) * CORES + core


def pairs(lags, rows, target):
    out = []
    for lag in range(lags):
        for row in range(rows):
            goal = target(lag, row)
            if goal is not None and 0 <= goal[0] < lags and 0 <= goal[1] < rows:
                out.append((lag * rows + row, goal[0] * rows + goal[1]))
    return out


def send(value, target):
    lags, rows = lax.axis_size("lag"), lax.axis_size("row")
    return lax.ppermute(value, AXES, pairs(lags, rows, target))


def along_z(step, when):
    def target(lag, row):
        z, x, core = coords(lag)
        return (lag_of(z + step, x, core), row) if when(z, x) and z + step >= 0 else None
    return target


def along_x(step, when):
    def target(lag, row):
        z, x, core = coords(lag)
        return (lag_of(z, x + step, core), row) if when(z, x) else None
    return target


def other_core(lag, row):
    return lag ^ 1, row


def sparse_row(z_ref, row, tile, cols, count):
    left = jnp.concatenate([z_ref[row, j] for j in range(count)], axis=1)
    right = jnp.concatenate([tile(cols(j)) for j in range(count)], axis=0)
    return jnp.dot(left, right, preferred_element_type=jnp.float32)


def low_lanes(shape):
    return lax.broadcasted_iota(jnp.int32, shape, len(shape) - 1) < HALF


def pack(first, second):
    low = low_lanes(first.shape)
    return (
        jnp.where(low, first, pltpu.roll(second, HALF, 1)),
        jnp.where(low, pltpu.roll(first, HALF, 1), second),
    )


VMEM = pl.BlockSpec(memory_space=pltpu.VMEM)
SMEM = pl.BlockSpec(memory_space=pltpu.SMEM)
CORE, ROOT, NEXT, HEAD = 0, 1, 2, 8


def call(kernel, out_shape, flops, meta, *args):
    outs = len(out_shape) if isinstance(out_shape, tuple) else 0
    return pl.pallas_call(
        kernel,
        out_shape=out_shape,
        in_specs=[SMEM] + [VMEM] * len(args),
        out_specs=(VMEM,) * outs if outs else VMEM,
        compiler_params=pltpu.CompilerParams(vmem_limit_bytes=14 * 1024 * 1024),
        cost_estimate=pl.CostEstimate(flops=flops, bytes_accessed=5 * 10 ** 6, transcendentals=0),
    )(meta, *args)


def history_kernel(meta, z_ref, *refs):
    pasts, (keep_ref, send_ref) = refs[:-2], refs[-2:]
    blocks, count, width, unused = z_ref.shape

    def tile(col):
        return jnp.concatenate([past[col] for past in pasts], axis=1)

    for pair in range(blocks // 2):
        rows = []
        for row in (2 * pair, 2 * pair + 1):
            base = HEAD + row * count
            rows.append(sparse_row(z_ref, row, tile, lambda j: meta[base + j], count))
        for number in range(len(pasts)):
            lanes = slice(number * width, (number + 1) * width)
            low, high = pack(*(row[:, lanes] for row in rows))
            place = number * (blocks // 2) + pair
            keep_ref[place] = jnp.where(meta[CORE] == 0, low, high)
            send_ref[place] = jnp.where(meta[CORE] == 0, high, low)


def history_partial(meta, zmat, *pasts):
    blocks, count, width, unused = zmat.shape
    half = jax.ShapeDtypeStruct((len(pasts) * blocks // 2, width, width), jnp.float32)
    return call(
        history_kernel, (half, half), 2 * len(pasts) * blocks * count * width ** 3,
        meta, zmat, *pasts,
    )


def packed_rows(meta, z_ref, now_ref, pair):
    count = z_ref.shape[1]
    rows = []
    for row in (2 * pair, 2 * pair + 1):
        base = HEAD + row * count

        def tile(col):
            both = now_ref[col // 2]
            mine = low_lanes(both.shape) == (col % 2 == 0)
            return jnp.where(mine, both, jnp.zeros_like(both))

        total = sparse_row(z_ref, row, tile, lambda j: meta[base + j], count)
        rows.append(total + pltpu.roll(total, HALF, 1))
    return jnp.where(low_lanes(rows[0].shape), rows[0], rows[1])


def lag_kernel(flag, meta, z_ref, now_ref, *rest):
    more, out_ref = rest[:-1], rest[-1]

    @pl.when(meta[flag] != 0)
    def _():
        for pair in range(out_ref.shape[0]):
            total = packed_rows(meta, z_ref, now_ref, pair)
            for ref in more:
                total = total + ref[pair].astype(jnp.float32)
            out_ref[pair] = total.astype(out_ref.dtype)


def lag_product(flag, dtype, meta, zmat, now, *more):
    blocks, count, width, unused = zmat.shape
    return call(
        functools.partial(lag_kernel, flag),
        jax.ShapeDtypeStruct((blocks // 2, width, width), dtype),
        2 * blocks * count * width ** 3, meta, zmat, now, *more,
    )


def step_kernel(place, meta, incident_ref, summed_ref, inverse_ref, *refs):
    out_ref = refs[-1]

    @pl.when(meta[ROOT] != 0)
    def _():
        for pair in range(out_ref.shape[0]):
            low, high = pack(*(incident_ref[2 * pair + p].astype(jnp.float32) for p in range(2)))
            driven = jnp.where(meta[CORE] == 0, low, high) - summed_ref[place * out_ref.shape[0] + pair]
            if len(refs) > 1:
                driven = driven - packed_rows(meta, refs[0], refs[1], pair)
            for old in refs[2:-1]:
                driven = driven - old[pair].astype(jnp.float32)
            solved = [
                jnp.dot(
                    inverse_ref[2 * pair + p], driven,
                    precision=lax.Precision.HIGHEST, preferred_element_type=jnp.float32,
                )
                for p in range(2)
            ]
            out_ref[pair] = jnp.where(low_lanes(driven.shape), *solved).astype(out_ref.dtype)


def solve_step(place, meta, incident, summed, inverse, *more):
    blocks, width, unused = inverse.shape
    return call(
        functools.partial(step_kernel, place),
        jax.ShapeDtypeStruct((blocks // 2, width, width), jnp.bfloat16),
        10 ** 9, meta, incident, summed, inverse, *more,
    )


def unpack_kernel(meta, mine_ref, other_ref, out_ref):
    for pair in range(mine_ref.shape[0]):
        mine, other = mine_ref[pair].astype(jnp.float32), other_ref[pair].astype(jnp.float32)
        low = jnp.where(meta[CORE] == 0, mine, other)
        high = jnp.where(meta[CORE] == 0, other, mine)
        first, second = pack(low, high)
        out_ref[2 * pair] = first.astype(out_ref.dtype)
        out_ref[2 * pair + 1] = second.astype(out_ref.dtype)


def unpack(meta, mine, other):
    count, width, unused = mine.shape
    return call(
        unpack_kernel, jax.ShapeDtypeStruct((2 * count, width, width), mine.dtype),
        10 ** 6, meta, mine, other,
    )


def swap_rows(lag, row):
    return lag, row ^ 1


def next_chip(lag, row):
    return lag, (row + 2 if row % 2 == 0 else row - 2)


def on_root(step):
    def target(lag, row):
        return (lag, row + step) if lag < CORES else None
    return target


def after(value, *done):
    return lax.optimization_barrier((value,) + done)[0]


TREE = (
    along_x(-1, lambda z, x: x % 2 == 1),
    along_x(-2, lambda z, x: x == 2),
    along_z(-1, lambda z, x: x == 0 and z % 2 == 1),
    along_z(-2, lambda z, x: x == 0 and z == 2),
)


def halves(pieces):
    keep, extra = pieces
    return keep + send(extra, other_core)


def stage(total, number):
    moved = send(total.astype(jnp.bfloat16), TREE[number])
    return total + moved.astype(jnp.float32)


def spread(value, got):
    moves = (
        along_z(2, lambda z, x: x == 0 and z == 0),
        along_z(1, lambda z, x: x == 0 and z % 2 == 0),
        along_x(2, lambda z, x: x == 0),
        along_x(1, lambda z, x: x % 2 == 0),
    )
    for move, here in zip(moves, got):
        value = jnp.where(here, send(value, move), value)
    return value


def per_device(z_blocks, block_cols, history, incident, near_inverse):
    blocks, width, unused = near_inverse.shape
    zmat = z_blocks[0]
    lag_pos = lax.axis_index("lag")
    row_pos = lax.axis_index("row")
    z_pos, x_pos, core = coords(lag_pos)
    own = history[0].reshape(blocks, width, width)
    fields = [f.reshape(blocks, width, width) for f in incident]

    cols = block_cols[0].reshape(-1) - (row_pos - 1) * blocks
    group, inside = cols // blocks, cols % blocks
    even = row_pos % 2 == 0
    slot = jnp.where(group == 1, 0, jnp.where((group == 2) == even, 1, 2))
    chip = lag_pos // CORES
    flags = jnp.stack([core, chip == 0, chip == 1] + [0] * (HEAD - 3)).astype(jnp.int32)
    history_meta = jnp.concatenate([flags, slot * blocks + inside])

    def first_chips(lag, row):
        return (lag ^ 1, row) if lag < 2 * CORES else None

    def next_lag(past):
        return send(past, lambda lag, row: (lag + 1, row))

    def wide(value):
        below = send(value, on_root(1))
        above = send(value, on_root(-1))
        return jnp.concatenate([below, value, above], axis=0)

    near = send(own, swap_rows)
    swapped_cols = send(cols, first_chips)
    swapped = send(zmat, first_chips)
    first = jnp.where(core == 0, zmat, swapped)
    second = jnp.where(core == 0, swapped, zmat)
    first_meta = jnp.concatenate([flags, jnp.where(core == 0, cols, swapped_cols)])
    second_meta = jnp.concatenate([flags, jnp.where(core == 0, swapped_cols, cols)])
    x_zero = x_pos == 0
    got = [x_zero & (z_pos == 2), x_zero & (z_pos % 2 == 1), x_pos == 2, x_pos % 2 == 1]
    near, history_meta, first_meta, second_meta, got, first, second = lax.optimization_barrier(
        (near, history_meta, first_meta, second_meta, got, first, second)
    )
    far = send(near, next_chip)
    past0 = jnp.concatenate([own, near, far], axis=0)
    past1 = next_lag(past0)

    def partial(past):
        return history_partial(history_meta, zmat, past)

    a = stage(halves(partial(past0)), 0)
    part1 = partial(past1)
    a = stage(after(a, part1[0]), 1)
    b = halves(part1)
    past2 = next_lag(after(past1, a))
    a = stage(after(a, b), 2)
    b = stage(b, 0)
    a = stage(after(a, b), 3)
    b = stage(b, 1)
    current0 = solve_step(0, first_meta, fields[0], after(a, b), near_inverse)
    part2 = partial(after(past2, current0))
    past3 = next_lag(after(past2, current0))
    c = halves(part2)

    b = stage(after(b, current0), 2)
    c0 = wide(current0)
    c = stage(after(c, current0), 0)
    part3 = partial(after(past3, current0))
    b = stage(b, 3)
    c = stage(c, 1)
    d = halves(part3)
    current1 = solve_step(0, first_meta, fields[1], after(b, d), near_inverse, first, c0)

    c = stage(after(c, current1), 2)
    d = stage(after(d, current1), 0)
    third = send(after(c0, current1), along_x(1, lambda z, x: z == 0 and x == 0))
    c1 = wide(current1)
    old = lag_product(ROOT, jnp.float32, second_meta, second, after(c0, c, d))
    c = stage(c, 3)
    d = stage(d, 1)
    third = lag_product(NEXT, jnp.bfloat16, first_meta, first, third)
    current2 = solve_step(0, first_meta, fields[2], c, near_inverse, first, c1, old)

    third = send(after(third, current2), along_x(-1, lambda z, x: z == 0 and x == 1))
    d = stage(after(d, current2), 2)
    c2 = wide(current2)
    old = lag_product(ROOT, jnp.float32, second_meta, second, after(c1, d))
    d = stage(d, 3)
    c3 = solve_step(0, first_meta, fields[3], d, near_inverse, first, c2, old, third)
    c3 = spread(c3, got)
    out = unpack(history_meta, c3, send(c3, other_core))
    return out.reshape(blocks * width, width)


def solution(mesh):
    return jax.shard_map(
        per_device,
        mesh=mesh,
        in_specs=(
            P("lag", "row", None, None, None),
            P("lag", "row", None),
            P("lag", "row", None),
            P(None, "row", None),
            P("row", None, None),
        ),
        out_specs=P("row", None),
        check_vma=False,
    )
```

```python
import functools

import jax
import jax.numpy as jnp
from jax import lax
from jax.experimental import pallas as pl
from jax.experimental.pallas import tpu as pltpu
from jax.sharding import PartitionSpec as P

CORES, XS = 2, 4
HALF = 64
AXES = ("lag", "row")


def coords(lag):
    return lag // (XS * CORES), lag // CORES % XS, lag % CORES


def lag_of(z, x, core):
    return (z * XS + x) * CORES + core


def pairs(lags, rows, target):
    out = []
    for lag in range(lags):
        for row in range(rows):
            goal = target(lag, row)
            if goal is not None and 0 <= goal[0] < lags and 0 <= goal[1] < rows:
                out.append((lag * rows + row, goal[0] * rows + goal[1]))
    return out


def send(value, target):
    lags, rows = lax.axis_size("lag"), lax.axis_size("row")
    return lax.ppermute(value, AXES, pairs(lags, rows, target))


def along_z(step, when):
    def target(lag, row):
        z, x, core = coords(lag)
        return (lag_of(z + step, x, core), row) if when(z, x) and z + step >= 0 else None
    return target


def along_x(step, when):
    def target(lag, row):
        z, x, core = coords(lag)
        return (lag_of(z, x + step, core), row) if when(z, x) else None
    return target


def other_core(lag, row):
    return lag ^ 1, row


def sparse_row(z_ref, row, tile, cols, count):
    left = jnp.concatenate([z_ref[row, j] for j in range(count)], axis=1)
    right = jnp.concatenate([tile(cols(j)) for j in range(count)], axis=0)
    return jnp.dot(left, right, preferred_element_type=jnp.float32)


def low_lanes(shape):
    return lax.broadcasted_iota(jnp.int32, shape, len(shape) - 1) < HALF


def pack(first, second):
    low = low_lanes(first.shape)
    return (
        jnp.where(low, first, pltpu.roll(second, HALF, 1)),
        jnp.where(low, pltpu.roll(first, HALF, 1), second),
    )


VMEM = pl.BlockSpec(memory_space=pltpu.VMEM)
SMEM = pl.BlockSpec(memory_space=pltpu.SMEM)
CORE, ROOT, NEXT, HEAD = 0, 1, 2, 8


def call(kernel, out_shape, flops, meta, *args):
    outs = len(out_shape) if isinstance(out_shape, tuple) else 0
    return pl.pallas_call(
        kernel,
        out_shape=out_shape,
        in_specs=[SMEM] + [VMEM] * len(args),
        out_specs=(VMEM,) * outs if outs else VMEM,
        compiler_params=pltpu.CompilerParams(vmem_limit_bytes=14 * 1024 * 1024),
        cost_estimate=pl.CostEstimate(flops=flops, bytes_accessed=5 * 10 ** 6, transcendentals=0),
    )(meta, *args)


def history_kernel(meta, z_ref, *refs):
    pasts, (keep_ref, send_ref) = refs[:-2], refs[-2:]
    blocks, count, width, unused = z_ref.shape

    def tile(col):
        return jnp.concatenate([past[col] for past in pasts], axis=1)

    for pair in range(blocks // 2):
        rows = []
        for row in (2 * pair, 2 * pair + 1):
            base = HEAD + row * count
            rows.append(sparse_row(z_ref, row, tile, lambda j: meta[base + j], count))
        for number in range(len(pasts)):
            lanes = slice(number * width, (number + 1) * width)
            low, high = pack(*(row[:, lanes] for row in rows))
            place = number * (blocks // 2) + pair
            keep_ref[place] = jnp.where(meta[CORE] == 0, low, high)
            send_ref[place] = jnp.where(meta[CORE] == 0, high, low)


def history_partial(meta, zmat, *pasts):
    blocks, count, width, unused = zmat.shape
    half = jax.ShapeDtypeStruct((len(pasts) * blocks // 2, width, width), jnp.float32)
    return call(
        history_kernel, (half, half), 2 * len(pasts) * blocks * count * width ** 3,
        meta, zmat, *pasts,
    )


def packed_rows(meta, z_ref, now_ref, pair):
    count = z_ref.shape[1]
    rows = []
    for row in (2 * pair, 2 * pair + 1):
        base = HEAD + row * count

        def tile(col):
            both = now_ref[col // 2]
            mine = low_lanes(both.shape) == (col % 2 == 0)
            return jnp.where(mine, both, jnp.zeros_like(both))

        total = sparse_row(z_ref, row, tile, lambda j: meta[base + j], count)
        rows.append(total + pltpu.roll(total, HALF, 1))
    return jnp.where(low_lanes(rows[0].shape), rows[0], rows[1])


def lag_kernel(flag, meta, z_ref, now_ref, *rest):
    more, out_ref = rest[:-1], rest[-1]

    @pl.when(meta[flag] != 0)
    def _():
        for pair in range(out_ref.shape[0]):
            total = packed_rows(meta, z_ref, now_ref, pair)
            for ref in more:
                total = total + ref[pair].astype(jnp.float32)
            out_ref[pair] = total.astype(out_ref.dtype)


def lag_product(flag, dtype, meta, zmat, now, *more):
    blocks, count, width, unused = zmat.shape
    return call(
        functools.partial(lag_kernel, flag),
        jax.ShapeDtypeStruct((blocks // 2, width, width), dtype),
        2 * blocks * count * width ** 3, meta, zmat, now, *more,
    )


def step_kernel(place, meta, incident_ref, summed_ref, inverse_ref, *refs):
    out_ref = refs[-1]

    @pl.when(meta[ROOT] != 0)
    def _():
        for pair in range(out_ref.shape[0]):
            low, high = pack(*(incident_ref[2 * pair + p].astype(jnp.float32) for p in range(2)))
            driven = jnp.where(meta[CORE] == 0, low, high) - summed_ref[place * out_ref.shape[0] + pair]
            if len(refs) > 1:
                driven = driven - packed_rows(meta, refs[0], refs[1], pair)
            for old in refs[2:-1]:
                driven = driven - old[pair].astype(jnp.float32)
            solved = [
                jnp.dot(
                    inverse_ref[2 * pair + p], driven,
                    precision=lax.Precision.HIGHEST, preferred_element_type=jnp.float32,
                )
                for p in range(2)
            ]
            out_ref[pair] = jnp.where(low_lanes(driven.shape), *solved).astype(out_ref.dtype)


def solve_step(place, meta, incident, summed, inverse, *more):
    blocks, width, unused = inverse.shape
    return call(
        functools.partial(step_kernel, place),
        jax.ShapeDtypeStruct((blocks // 2, width, width), jnp.bfloat16),
        10 ** 9, meta, incident, summed, inverse, *more,
    )


def unpack_kernel(meta, mine_ref, other_ref, out_ref):
    for pair in range(mine_ref.shape[0]):
        mine, other = mine_ref[pair].astype(jnp.float32), other_ref[pair].astype(jnp.float32)
        low = jnp.where(meta[CORE] == 0, mine, other)
        high = jnp.where(meta[CORE] == 0, other, mine)
        first, second = pack(low, high)
        out_ref[2 * pair] = first.astype(out_ref.dtype)
        out_ref[2 * pair + 1] = second.astype(out_ref.dtype)


def unpack(meta, mine, other):
    count, width, unused = mine.shape
    return call(
        unpack_kernel, jax.ShapeDtypeStruct((2 * count, width, width), mine.dtype),
        10 ** 6, meta, mine, other,
    )


def swap_rows(lag, row):
    return lag, row ^ 1


def next_chip(lag, row):
    return lag, (row + 2 if row % 2 == 0 else row - 2)


def on_root(step):
    def target(lag, row):
        return (lag, row + step) if lag < CORES else None
    return target


def after(value, *done):
    return lax.optimization_barrier((value,) + done)[0]


TREE = (
    along_x(-1, lambda z, x: x % 2 == 1),
    along_x(-2, lambda z, x: x == 2),
    along_z(-1, lambda z, x: x == 0 and z % 2 == 1),
    along_z(-2, lambda z, x: x == 0 and z == 2),
)


def halves(pieces):
    keep, extra = pieces
    return keep + send(extra, other_core)


def stage(total, number):
    moved = send(total.astype(jnp.bfloat16), TREE[number])
    return total + moved.astype(jnp.float32)


def spread(value, got):
    moves = (
        along_z(2, lambda z, x: x == 0 and z == 0),
        along_z(1, lambda z, x: x == 0 and z % 2 == 0),
        along_x(2, lambda z, x: x == 0),
        along_x(1, lambda z, x: x % 2 == 0),
    )
    for move, here in zip(moves, got):
        value = jnp.where(here, send(value, move), value)
    return value


def per_device(z_blocks, block_cols, history, incident, near_inverse):
    blocks, width, unused = near_inverse.shape
    zmat = z_blocks[0]
    lag_pos = lax.axis_index("lag")
    row_pos = lax.axis_index("row")
    z_pos, x_pos, core = coords(lag_pos)
    own = history[0].reshape(blocks, width, width)
    fields = [f.reshape(blocks, width, width) for f in incident]

    cols = block_cols[0].reshape(-1) - (row_pos - 1) * blocks
    group, inside = cols // blocks, cols % blocks
    even = row_pos % 2 == 0
    slot = jnp.where(group == 1, 0, jnp.where((group == 2) == even, 1, 2))
    chip = lag_pos // CORES
    flags = jnp.stack([core, chip == 0, chip == 1] + [0] * (HEAD - 3)).astype(jnp.int32)
    history_meta = jnp.concatenate([flags, slot * blocks + inside])

    def first_chips(lag, row):
        return (lag ^ 1, row) if lag < 2 * CORES else None

    def next_lag(past):
        return send(past, lambda lag, row: (lag + 1, row))

    def wide(value):
        below = send(value, on_root(1))
        above = send(value, on_root(-1))
        return jnp.concatenate([below, value, above], axis=0)

    near = send(own, swap_rows)
    swapped_cols = send(cols, first_chips)
    swapped = send(zmat, first_chips)
    first = jnp.where(core == 0, zmat, swapped)
    second = jnp.where(core == 0, swapped, zmat)
    first_meta = jnp.concatenate([flags, jnp.where(core == 0, cols, swapped_cols)])
    second_meta = jnp.concatenate([flags, jnp.where(core == 0, swapped_cols, cols)])
    x_zero = x_pos == 0
    got = [x_zero & (z_pos == 2), x_zero & (z_pos % 2 == 1), x_pos == 2, x_pos % 2 == 1]
    near, history_meta, first_meta, second_meta, got, first, second = lax.optimization_barrier(
        (near, history_meta, first_meta, second_meta, got, first, second)
    )
    far = send(near, next_chip)
    past0 = jnp.concatenate([own, near, far], axis=0)
    past1 = next_lag(past0)
    past2 = next_lag(past1)
    past3 = next_lag(past2)

    def partial(past):
        return history_partial(history_meta, zmat, past)

    a = stage(halves(partial(past0)), 0)
    part1 = partial(past1)
    a = stage(after(a, part1[0]), 1)
    b = halves(part1)
    a = stage(after(a, b), 2)
    b = stage(b, 0)
    part2 = partial(after(past2, a))
    a = stage(after(a, b), 3)
    b = stage(b, 1)
    c = halves(part2)
    current0 = solve_step(0, first_meta, fields[0], after(a, b, part2[0]), near_inverse)

    b = stage(after(b, current0), 2)
    c0 = wide(current0)
    c = stage(after(c, current0), 0)
    part3 = partial(after(past3, current0))
    b = stage(b, 3)
    c = stage(c, 1)
    d = halves(part3)
    current1 = solve_step(0, first_meta, fields[1], after(b, c, d), near_inverse, first, c0)

    c = stage(after(c, current1), 2)
    d = stage(after(d, current1), 0)
    c1 = wide(current1)
    third = send(after(c0, current1), along_x(1, lambda z, x: z == 0 and x == 0))
    old = lag_product(ROOT, jnp.float32, second_meta, second, after(c0, c, d))
    c = stage(c, 3)
    d = stage(d, 1)
    current2 = solve_step(0, first_meta, fields[2], after(c, d), near_inverse, first, c1, old)

    third = lag_product(NEXT, jnp.bfloat16, first_meta, first, third)
    third = send(after(third, current2), along_x(-1, lambda z, x: z == 0 and x == 1))
    d = stage(after(d, current2), 2)
    c2 = wide(current2)
    old = lag_product(ROOT, jnp.float32, second_meta, second, after(c1, d))
    d = stage(d, 3)
    c3 = solve_step(0, first_meta, fields[3], d, near_inverse, first, c2, old, third)
    c3 = spread(c3, got)
    out = unpack(history_meta, c3, send(c3, other_core))
    return out.reshape(blocks * width, width)


def solution(mesh):
    return jax.shard_map(
        per_device,
        mesh=mesh,
        in_specs=(
            P("lag", "row", None, None, None),
            P("lag", "row", None),
            P("lag", "row", None),
            P(None, "row", None),
            P("row", None, None),
        ),
        out_specs=P("row", None),
        check_vma=False,
    )
```
